512 devices in a mesh: region: 128 (over x, z, core), slab: 4 (over y).
Axes of the slice: x: 4, y: 4, z: 16, core: 2. Of those that a mesh axis runs over, the one named last changes fastest.
Arguments:
- features: bfloat16 [13312, 4, 4, 4, 128], P(('region', 'slab')), may hold values from -6 to 6
- weight: bfloat16 [27, 128, 128], replicated, may hold values from -0.109375 to 0.109375
- cotangent: bfloat16 [13312, 4, 4, 4, 128], P(('region', 'slab')), may hold values from -6 to 6
- occupancy: int32 [13312, 64], P(('region', 'slab')), may hold values 0 or 1
- neighbors: int32 [13312, 6], P(('region', 'slab')), may hold values from -1 to 13311, as said below
Outputs:
- output: bfloat16 [13312, 4, 4, 4, 128], P(('region', 'slab'))
- input_grad: bfloat16 [13312, 4, 4, 4, 128], P(('region', 'slab'))
- weight_grad: float32 [27, 128, 128], replicated
The draws below stay inside these ranges and needn't reach their ends.
Inputs may be any that keep to these rules, and one draw needn't show every extreme that they name: `neighbors`: links are mutual: if the +d entry of brick a is b, the -d entry of b is a. A third-dimension entry names the brick with the same position in its device's block on the device one slab index lower or higher. Every first- and second-dimension entry names a brick of a device with the same slab index and a region index that differs by a step of 1 to 64 modulo 128; for a given slab index, dimension and sender's brick position that step is the same on every region index. One device sends at most 2 first- and second-dimension faces to any other device, and that many is reached.
All inputs are finite; a program needn't handle non-finite values. No bound on the sum of `occupancy` on one device may be relied on, other than what follows from the above.
Results may differ from the reference program's by a relative error of at most 0.0029.
Values may be sent and summed in bfloat16 or wider, within the bound.
A program may use at most 64 MiB of HBM per device.

```python
import jax
import jax.numpy as jnp
from jax import lax

C = 128
EDGE = 4
BRICKS_DEV = 26
BRICKS = 13312
HALF = 64
N_REGION = 128
N_SLAB = 4


def draw_neighbors(key, part):
    key = jax.random.fold_in(key, 11)
    key_list = jax.random.split(key, 4)
    class_keys = jax.random.split(key_list[0], N_SLAB)
    classes = jax.vmap(lambda single: jax.random.permutation(single, HALF - 2))(class_keys).astype(jnp.int32)
    link_ids = jnp.arange(2 * BRICKS_DEV, dtype=jnp.int32)
    spread_steps = 2 + classes[:, (link_ids - 2) % (HALF - 2)]
    forced = jnp.where(link_ids == 0, HALF, 1).astype(jnp.int32)
    offsets = jnp.where((link_ids < 2)[None, :], forced[None, :], spread_steps).reshape(N_SLAB, 2, BRICKS_DEV)
    shuffle_keys = jax.random.split(key_list[1], N_SLAB * 2)
    shuffles = jax.vmap(lambda single: jax.random.permutation(single, BRICKS_DEV))(shuffle_keys).astype(jnp.int32).reshape(N_SLAB, 2, BRICKS_DEV)
    region_ids = jnp.arange(N_REGION, dtype=jnp.int32)[:, None, None, None]
    slab_ids = jnp.arange(N_SLAB, dtype=jnp.int32)[None, :, None, None]
    brick_ids = jnp.arange(BRICKS_DEV, dtype=jnp.int32)[None, None, None, :]
    sources = (region_ids * N_SLAB + slab_ids) * BRICKS_DEV + brick_ids + jnp.zeros((1, 1, 2, 1), jnp.int32)
    targets = ((region_ids + offsets[None]) % N_REGION * N_SLAB + slab_ids) * BRICKS_DEV + shuffles[None]
    table = jnp.full((BRICKS, 6), -1, jnp.int32)
    for axis_number in range(2):
        source_flat = sources[:, :, axis_number].reshape(-1)
        target_flat = targets[:, :, axis_number].reshape(-1)
        table = table.at[source_flat, 2 * axis_number + 1].set(target_flat)
        table = table.at[target_flat, 2 * axis_number].set(source_flat)
    keep_third = jax.random.randint(key_list[3], (N_REGION, N_SLAB, BRICKS_DEV), 0, 4) > 0
    slab_grid = jnp.arange(N_SLAB, dtype=jnp.int32)[None, :, None]
    lower_ids = (jnp.arange(N_REGION, dtype=jnp.int32)[:, None, None] * N_SLAB + slab_grid) * BRICKS_DEV + jnp.arange(BRICKS_DEV, dtype=jnp.int32)[None, None, :]
    upward = keep_third & (slab_grid + 1 < N_SLAB)
    upper_ids = lower_ids + BRICKS_DEV
    table = table.at[lower_ids.reshape(-1), 5].set(jnp.where(upward, upper_ids, -1).reshape(-1))
    table = table.at[jnp.where(upward, upper_ids, BRICKS).reshape(-1), 4].set(lower_ids.reshape(-1), mode='drop')
    return table


def with_ends(drawn, own_key, smallest, high):
    extent = drawn.shape
    place = [jax.random.randint(jax.random.fold_in(own_key, axis), (), 0, extent[axis]) for axis in range(len(extent))]
    drawn = drawn.at[tuple(place)].set(smallest)
    longest = extent.index(max(extent))
    place[longest] = (place[longest] + 1) % extent[longest]
    return drawn.at[tuple(place)].set(high)


def block_levels(stream_key, extent, cuts, smallest, top_value):
    gain, own = 1.0, jax.random.fold_in(stream_key, 6)
    for axis_at, shards_of in cuts:
        steps = jnp.exp(jax.random.uniform(jax.random.fold_in(own, axis_at), (shards_of,), jnp.float32, smallest / len(cuts), top_value / len(cuts)))
        gain = gain * jnp.repeat(steps, extent[axis_at] // shards_of).reshape([-1 if axis == axis_at else 1 for axis in range(len(extent))])
    return gain


def normal_values(key, shape, spread, reach, cuts=(), kind=jnp.bfloat16):
    factor_of = block_levels(key, shape, cuts, -0.22, 0.18) if cuts else 1.0
    drawn = jax.random.normal(key, shape, jnp.float32) * spread * factor_of
    return jnp.minimum(jnp.maximum(drawn, -reach), reach).astype(kind)


def setup_inputs(seed: int = 0) -> dict:
    seeds = jax.random.split(jax.random.key(seed), 6)
    return {
        "features": normal_values(seeds[0], (BRICKS, EDGE, EDGE, EDGE, C), 1.0, 6.0, ((0, 512),)),
        "weight": normal_values(seeds[1], (27, C, C), (27 * C) ** -0.5, 0.109375),
        "cotangent": normal_values(seeds[2], (BRICKS, EDGE, EDGE, EDGE, C), 1.0, 6.0, ((0, 512),)),
        "occupancy": with_ends((jax.random.randint(seeds[3], (BRICKS, EDGE * EDGE * EDGE), 0, 4) < 3).astype(jnp.int32), jax.random.fold_in(seeds[3], 1), 0, 1),
        "neighbors": draw_neighbors(jax.random.fold_in(seeds[5], 71), 0),
    }


def face_pads(source, neighbors):
    faces = (source[:, 0], source[:, -1], source[:, :, 0], source[:, :, -1], source[:, :, :, 0], source[:, :, :, -1])
    collected = []
    for side in range(6):
        column = neighbors[:, side]
        safe_ids = jnp.maximum(column, 0)
        taken = faces[side ^ 1][safe_ids]
        collected.append(jnp.where((column >= 0)[:, None, None, None], taken, jnp.zeros_like(taken)))
    return jnp.stack(collected, axis=1)


def assemble_brick(core, planes):
    z_rim = ((0, 0), (0, 0), (1, 1), (0, 0))
    xy_rim = ((0, 0), (1, 1), (1, 1), (0, 0))
    stacked = jnp.concatenate([planes[:, 4][:, :, :, None], core, planes[:, 5][:, :, :, None]], axis=3)
    lower_y = jnp.pad(planes[:, 2], z_rim)[:, :, None]
    upper_y = jnp.pad(planes[:, 3], z_rim)[:, :, None]
    middle = jnp.concatenate([lower_y, stacked, upper_y], axis=2)
    lower_x = jnp.pad(planes[:, 0], xy_rim)[:, None]
    upper_x = jnp.pad(planes[:, 1], xy_rim)[:, None]
    return jnp.concatenate([lower_x, middle, upper_x], axis=1)


def convolve(padded, kernel):
    bricks_here = padded.shape[0]
    channels = padded.shape[-1]
    edge = padded.shape[1] - 2
    accumulated = jnp.zeros((bricks_here * edge ** 3, kernel.shape[-1]), jnp.float32)
    for tap_index in range(27):
        first_offset, second_offset, third_offset = tap_index // 9, tap_index // 3 % 3, tap_index % 3
        window = padded[:, first_offset:first_offset + edge, second_offset:second_offset + edge, third_offset:third_offset + edge].reshape(-1, channels)
        accumulated = accumulated + jnp.dot(window, kernel[tap_index], preferred_element_type=jnp.float32)
    return accumulated.reshape(bricks_here, edge, edge, edge, -1)


def reference(features, weight, cotangent, occupancy, neighbors):
    total_bricks = features.shape[0]
    channels = features.shape[-1]
    edge = features.shape[1]
    groups = total_bricks // BRICKS_DEV
    flipped = jnp.swapaxes(weight[::-1], 1, 2)
    occupied = occupancy.astype(jnp.float32).reshape(total_bricks, edge, edge, edge, 1)
    feature_pads = face_pads(features, neighbors)

    def grouped(array):
        return array.reshape((groups, BRICKS_DEV) + array.shape[1:])

    def forward_group(inputs):
        core, planes, mask_part, grad_part = inputs
        pre = convolve(assemble_brick(core, planes), weight)
        sigma = jax.nn.sigmoid(pre)
        result = (core.astype(jnp.float32) + mask_part * pre * sigma).astype(jnp.bfloat16)
        pre_grad = (grad_part.astype(jnp.float32) * mask_part * sigma * (1.0 + pre * (1.0 - sigma))).astype(jnp.bfloat16)
        return result, pre_grad

    output, pre_grad = lax.map(forward_group, (grouped(features), grouped(feature_pads), grouped(occupied), grouped(cotangent)))
    output = output.reshape(features.shape)
    pre_grad = pre_grad.reshape(features.shape)
    grad_pads = face_pads(pre_grad, neighbors)

    def backward_group(carried, inputs):
        core, planes, grad_core, grad_planes, upstream = inputs
        back = convolve(assemble_brick(grad_core, grad_planes), flipped)
        input_grad = (upstream.astype(jnp.float32) + back).astype(jnp.bfloat16)
        padded = assemble_brick(core, planes)
        flat_grad = grad_core.reshape(-1, channels)
        pieces = []
        for tap_index in range(27):
            first_offset, second_offset, third_offset = tap_index // 9, tap_index // 3 % 3, tap_index % 3
            window = padded[:, first_offset:first_offset + edge, second_offset:second_offset + edge, third_offset:third_offset + edge].reshape(-1, channels)
            pieces.append(jnp.dot(window.T, flat_grad, preferred_element_type=jnp.float32))
        return carried + jnp.stack(pieces, axis=0), input_grad

    initial = jnp.zeros((27, channels, channels), jnp.float32)
    summed, input_grad = lax.scan(backward_group, initial, (grouped(features), grouped(feature_pads), grouped(pre_grad), grouped(grad_pads), grouped(cotangent)))
    weight_grad = summed * (total_bricks * float(edge ** 3)) ** -0.5
    return output, input_grad.reshape(features.shape), weight_grad
```

```python
import functools

import jax
import jax.numpy as jnp
from jax import lax
from jax.experimental import pallas as pl
from jax.experimental.pallas import tpu as pltpu
from jax.sharding import PartitionSpec as P

MESH = pl.DeviceIdType.MESH
BF = jnp.bfloat16
F32 = jnp.float32

CH = 128
BD = 26
BP = 32
VOX = 64
REG = 128
SLB = 4
NX, NZ, NCORE = 4, 16, 2
NXY = NX * SLB
SLOTS = 2 * REG
TAPS = 27
TPAD = 32
HALF_T = TPAD // 2
VMEM_LIMIT = 50 * 1024 * 1024


def params(**kw):
    return pltpu.CompilerParams(vmem_limit_bytes=VMEM_LIMIT, **kw)


def vmem(shape, dtype):
    return jax.ShapeDtypeStruct(shape, dtype)


IN_VMEM = pl.BlockSpec(memory_space=pltpu.VMEM)
IN_SMEM = pl.BlockSpec(memory_space=pltpu.SMEM)
IN_ANY = pl.BlockSpec(memory_space=pl.ANY)


def face_voxels(side):
    if side == 0:
        return [4 * a + b for a in range(4) for b in range(4)]
    if side == 1:
        return [48 + 4 * a + b for a in range(4) for b in range(4)]
    if side == 2:
        return [16 * a + b for a in range(4) for b in range(4)]
    return [16 * a + 12 + b for a in range(4) for b in range(4)]


def fill_faces(slabs, faces):
    for side in range(4):
        for t, v in enumerate(face_voxels(side)):
            faces[side, pl.ds(t, BP, stride=16), :] = slabs(v)


def pack_slots(faces, slot_ref, slots):
    for side in range(4):

        def body(b, carry):
            slot = slot_ref[side * BD + b]
            tile = faces[side, pl.ds(pl.multiple_of(b * 16, 16), 16), :]
            slots[pl.ds(pl.multiple_of(slot * 16, 16), 16), :] = tile.astype(BF)
            return carry

        lax.fori_loop(0, BD, body, 0)


def pack_kernel(feat, slot_ref, x_ref, slots, rows, faces):
    rows[0 : BD * VOX, :] = feat[...].astype(F32)
    rows[BD * VOX :, :] = jnp.zeros((BP * VOX - BD * VOX, CH), F32)
    for v in range(VOX):
        x_ref[v] = rows[pl.ds(v, BP, stride=VOX), :].astype(BF)
    fill_faces(lambda v: rows[pl.ds(v, BP, stride=VOX), :], faces)
    pack_slots(faces, slot_ref, slots)


def exchange_start(me, slab, slots, recv, x_ref, low, high, sems):
    send_sem, recv_sem, z_send, z_recv = sems
    up = lax.rem(slab + 1, SLB)
    down = lax.rem(slab + SLB - 1, SLB)
    to_up = pltpu.make_async_remote_copy(
        x_ref.at[:, 3], low, z_send.at[0], z_recv.at[0],
        device_id={"region": me, "slab": up}, device_id_type=MESH)
    to_down = pltpu.make_async_remote_copy(
        x_ref.at[:, 0], high, z_send.at[1], z_recv.at[1],
        device_id={"region": me, "slab": down}, device_id_type=MESH)

    def send(k, carry):
        peer = lax.rem(me + k, REG)
        pltpu.make_async_remote_copy(
            slots.at[pl.ds(pl.multiple_of(peer * 32, 32), 32)],
            recv.at[pl.ds(pl.multiple_of(me * 32, 32), 32)],
            send_sem, recv_sem,
            device_id={"region": peer, "slab": slab}, device_id_type=MESH,
        ).start()
        return carry

    lax.fori_loop(1, REG, send, 0)
    to_up.start()
    to_down.start()
    return to_up, to_down


def exchange_wait(slots, recv, sems, pair):
    send_sem, recv_sem, _, _ = sems
    span = pl.ds(0, (REG - 1) * 32)
    pltpu.make_async_copy(recv.at[span], recv.at[span], recv_sem).wait()
    pltpu.make_async_copy(slots.at[span], slots.at[span], send_sem).wait()
    for copy in pair:
        copy.wait()


def region_barrier(me, slab, barrier):
    def greet(k, carry):
        pl.semaphore_signal(
            barrier, inc=1, device_id={"region": lax.rem(me + k, REG), "slab": slab},
            device_id_type=MESH)
        return carry

    lax.fori_loop(1, REG, greet, 0)


def first_exchange(slots, x_ref, recv, low, high, send_sem, recv_sem, z_send, z_recv):
    me = lax.axis_index("region")
    slab = lax.axis_index("slab")
    barrier = pltpu.get_barrier_semaphore()
    region_barrier(me, slab, barrier)
    for step in (1, SLB - 1):
        pl.semaphore_signal(
            barrier, inc=1, device_id={"region": me, "slab": lax.rem(slab + step, SLB)},
            device_id_type=MESH)
    pl.semaphore_wait(barrier, REG - 1 + 2)
    sems = (send_sem, recv_sem, z_send, z_recv)
    pair = exchange_start(me, slab, slots, recv, x_ref, low, high, sems)
    exchange_wait(slots, recv, sems, pair)


def second_exchange(slots, x_ref, grad, recv, low, high, total, part, col, mine, got0, got1, got2,
                    send_sem, recv_sem, z_send, z_recv, a_sem, b_sem, c_sem, d_sem, e_sem, f_sem):
    me = lax.axis_index("region")
    slab = lax.axis_index("slab")
    x = me // (NZ * NCORE)
    z = lax.rem(me // NCORE, NZ)
    core = lax.rem(me, NCORE)
    q = x * SLB + slab

    def region_of(xx, zz, cc):
        return (xx * NZ + zz) * NCORE + cc

    def xy_peer(k):
        other = lax.rem(q + k, NXY)
        return other, {"region": region_of(other // SLB, z, core), "slab": lax.rem(other, SLB)}

    def z_peer(k):
        other = lax.rem(z + k, NZ)
        return other, {"region": region_of(x, other, core), "slab": slab}

    partner = {"region": region_of(x, z, 1 - core), "slab": slab}

    barrier = pltpu.get_barrier_semaphore()
    region_barrier(me, slab, barrier)

    def greet(k, carry):
        s = lax.rem(slab + 1 + lax.rem(k, SLB - 1), SLB)
        pl.semaphore_signal(
            barrier, inc=1, device_id={"region": region_of(k // (SLB - 1), z, core), "slab": s},
            device_id_type=MESH)
        return carry

    lax.fori_loop(0, NX * (SLB - 1), greet, 0)
    pl.semaphore_wait(barrier, REG - 1 + NX * (SLB - 1))

    own = pl.ds(pl.multiple_of(core * HALF_T, HALF_T), HALF_T)
    other_half = pl.ds(pl.multiple_of((1 - core) * HALF_T, HALF_T), HALF_T)
    pair0 = pltpu.make_async_remote_copy(
        grad.at[other_half], got0, a_sem.at[0], a_sem.at[1], device_id=partner, device_id_type=MESH)
    pair0.start()
    sems = (send_sem, recv_sem, z_send, z_recv)
    zpair = exchange_start(me, slab, slots, recv, x_ref, low, high, sems)
    pair0.wait()

    def add_pair(t, carry):
        part[t] = grad[core * HALF_T + t] + got0[t]
        return carry

    lax.fori_loop(0, HALF_T, add_pair, 0)

    def send1(k, carry):
        other, device = xy_peer(k)
        pltpu.make_async_remote_copy(
            part.at[:, pl.ds(pl.multiple_of(other * 8, 8), 8)], got1.at[q],
            b_sem.at[0], b_sem.at[1], device_id=device, device_id_type=MESH).start()
        return carry

    lax.fori_loop(1, NXY, send1, 0)
    got1[q] = part[:, pl.ds(pl.multiple_of(q * 8, 8), 8), :]
    span1 = got1.at[pl.ds(0, NXY - 1)]
    pltpu.make_async_copy(span1, span1, b_sem.at[1]).wait()
    pltpu.make_async_copy(span1, span1, b_sem.at[0]).wait()
    acc = got1[0]
    for k in range(1, NXY):
        acc = acc + got1[k]
    col[...] = acc

    def send2(k, carry):
        other, device = z_peer(k)
        pltpu.make_async_remote_copy(
            col.at[other], got2.at[z],
            c_sem.at[0], c_sem.at[1], device_id=device, device_id_type=MESH).start()
        return carry

    lax.fori_loop(1, NZ, send2, 0)
    got2[z] = col[z]
    span2 = got2.at[pl.ds(0, NZ - 1)]
    pltpu.make_async_copy(span2, span2, c_sem.at[1]).wait()
    pltpu.make_async_copy(span2, span2, c_sem.at[0]).wait()
    acc = got2[0]
    for k in range(1, NZ):
        acc = acc + got2[k]

    mine[z] = acc

    def send3(k, carry):
        _, device = z_peer(k)
        pltpu.make_async_remote_copy(
            mine.at[z], mine.at[z],
            d_sem.at[0], d_sem.at[1], device_id=device, device_id_type=MESH).start()
        return carry

    lax.fori_loop(1, NZ, send3, 0)
    span3 = mine.at[pl.ds(0, NZ - 1)]
    pltpu.make_async_copy(span3, span3, d_sem.at[1]).wait()
    pltpu.make_async_copy(span3, span3, d_sem.at[0]).wait()

    rows = pl.ds(pl.multiple_of(q * 8, 8), 8)

    def send4(k, carry):
        _, device = xy_peer(k)
        pltpu.make_async_remote_copy(
            mine, total.at[own, rows],
            e_sem.at[0], e_sem.at[1], device_id=device, device_id_type=MESH).start()
        return carry

    lax.fori_loop(1, NXY, send4, 0)
    total[own, rows, :] = mine[...]
    span4 = got1.at[pl.ds(0, NXY - 1)]
    pltpu.make_async_copy(span4, span4, e_sem.at[1]).wait()
    pltpu.make_async_copy(span4, span4, e_sem.at[0]).wait()

    pair1 = pltpu.make_async_remote_copy(
        total.at[own], total.at[own], f_sem.at[0], f_sem.at[1], device_id=partner, device_id_type=MESH)
    pair1.start()
    exchange_wait(slots, recv, sems, zpair)
    pair1.wait()


def build_halo(pad, x_ref, recv, slot_ref, low, high, lkeep, hkeep, faces):
    for a in (0, 5):
        for b in (0, 5):
            for c in range(6):
                pad[a, b, c] = jnp.zeros((BP, CH), BF)
                if 0 < c < 5:
                    pad[a, c, b] = jnp.zeros((BP, CH), BF)
                    pad[c, a, b] = jnp.zeros((BP, CH), BF)
    for i in range(4):
        for j in range(4):
            for k in range(4):
                pad[i + 1, j + 1, k + 1] = x_ref[4 * i + j, k]
            pad[i + 1, j + 1, 0] = (low[4 * i + j].astype(F32) * lkeep[...]).astype(BF)
            pad[i + 1, j + 1, 5] = (high[4 * i + j].astype(F32) * hkeep[...]).astype(BF)
    for side in range(4):
        faces[side, BD * 16 :, :] = jnp.zeros(((BP - BD) * 16, CH), F32)

        def body(b, carry):
            slot = slot_ref[side * BD + b]
            safe = jnp.maximum(slot, 0)
            tile = recv[pl.ds(pl.multiple_of(safe * 16, 16), 16), :].astype(F32)
            faces[side, pl.ds(pl.multiple_of(b * 16, 16), 16), :] = jnp.where(slot >= 0, tile, 0.0)
            return carry

        lax.fori_loop(0, BD, body, 0)
        for a in range(4):
            for b in range(4):
                slab = faces[side, pl.ds(4 * a + b, BP, stride=16), :].astype(BF)
                if side < 2:
                    pad[5 * side, a + 1, b + 1] = slab
                else:
                    pad[a + 1, 5 * (side - 2), b + 1] = slab


def conv_plane(pad, w_ref, plane):
    acc = None
    for o1 in range(3):
        for o2 in range(3):
            lhs = jnp.concatenate(
                [pad[plane + o1, o2 : o2 + 4, o3 : o3 + 4].reshape(16 * BP, CH) for o3 in range(3)],
                axis=1)
            tap = 9 * o1 + 3 * o2
            term = jnp.dot(lhs, w_ref[tap * CH : (tap + 3) * CH, :], preferred_element_type=F32)
            acc = term if acc is None else acc + term
    return acc


def forward_kernel(x_ref, recv, low, high, recv_slot, send_slot, lkeep, hkeep, w_ref, cot, occ,
                   out, g_ref, slots, grad, pad, faces, rows, outs, gt):
    build_halo(pad, x_ref, recv, recv_slot, low, high, lkeep, hkeep, faces)
    rows[0 : BD * VOX, :] = cot[...].astype(F32)
    rows[BD * VOX :, :] = jnp.zeros((BP * VOX - BD * VOX, CH), F32)

    def plane_body(plane, carry):
        pre = conv_plane(pad, w_ref, plane)
        mask = occ[plane]
        for t in range(16):
            u = pre[t * BP : (t + 1) * BP, :]
            s = 1.0 / (1.0 + jnp.exp(-u))
            m = mask[:, t : t + 1]
            f = x_ref[4 * plane + t // 4, t % 4].astype(F32)
            c = rows[pl.ds(16 * plane + t, BP, stride=VOX), :]
            outs[pl.ds(16 * plane + t, BP, stride=VOX), :] = f + m * (u * s)
            g_ref[4 * plane + t // 4, t % 4] = (c * m * s * (1.0 + u * (1.0 - s))).astype(BF)
        return carry

    lax.fori_loop(0, 4, plane_body, 0)
    out[...] = outs[0 : BD * VOX, :].astype(BF)
    fill_faces(lambda v: g_ref[v // 4, v % 4].astype(F32), faces)
    pack_slots(faces, send_slot, slots)
    for k in range(16):
        gt[:, 128 * k : 128 * (k + 1)] = g_ref[k].reshape(128, CH).T

    def tap_body(n, carry):
        o1 = n // 3
        o2 = lax.rem(n, 3)
        rhs = jnp.concatenate(
            [pad[pl.ds(o1, 4), pl.ds(o2, 4), o3 : o3 + 4].reshape(VOX * BP, CH) for o3 in range(3)],
            axis=1)
        res = jnp.dot(gt[...], rhs, preferred_element_type=F32)
        for o3 in range(3):
            grad[3 * n + o3] = res[:, CH * o3 : CH * (o3 + 1)].T
        return carry

    lax.fori_loop(0, 9, tap_body, 0)
    for t in range(TAPS, TPAD):
        grad[t] = jnp.zeros((CH, CH), F32)


def backward_kernel(g_ref, recv, low, high, recv_slot, lkeep, hkeep, w_ref, cot, out, pad, faces, rows, outs):
    build_halo(pad, g_ref, recv, recv_slot, low, high, lkeep, hkeep, faces)
    rows[0 : BD * VOX, :] = cot[...].astype(F32)
    rows[BD * VOX :, :] = jnp.zeros((BP * VOX - BD * VOX, CH), F32)

    def plane_body(plane, carry):
        back = conv_plane(pad, w_ref, plane)
        for t in range(16):
            c = rows[pl.ds(16 * plane + t, BP, stride=VOX), :]
            outs[pl.ds(16 * plane + t, BP, stride=VOX), :] = c + back[t * BP : (t + 1) * BP, :]
        return carry

    lax.fori_loop(0, 4, plane_body, 0)
    out[...] = outs[0 : BD * VOX, :].astype(BF)


def slot_tables(neighbors, me):
    linked = neighbors.T[:4].reshape(4 * BD)
    present = linked >= 0
    owner = jnp.where(present, linked // (BD * SLB), -1)
    position = linked % BD
    key = jnp.arange(4 * BD, dtype=jnp.int32)
    side = key // BD
    wanted = (side + 1 - 2 * (side % 2)) * BD + position
    same = owner[:, None] == owner[None, :]
    send_rank = jnp.sum(same & (key[None, :] < key[:, None]), axis=1, dtype=jnp.int32)
    recv_rank = jnp.sum(same & (wanted[None, :] < wanted[:, None]), axis=1, dtype=jnp.int32)
    send_slot = jnp.where(present, owner * 2 + send_rank, 2 * me)
    recv_slot = jnp.where(present, owner * 2 + recv_rank, -1)
    return send_slot, recv_slot


def shards(features, weight, cotangent, occupancy, neighbors):
    me = lax.axis_index("region")
    send_slot, recv_slot = slot_tables(neighbors, me)
    keep = (neighbors[:, 4:6] >= 0).astype(F32)
    keep = jnp.pad(keep, ((0, BP - BD), (0, 0)))
    lkeep, hkeep = keep[:, 0:1], keep[:, 1:2]
    occ = jnp.pad(occupancy.astype(F32), ((0, BP - BD), (0, 0))).reshape(BP, 4, 16).swapaxes(0, 1)
    feat = features.reshape(BD * VOX, CH)
    cot = cotangent.reshape(BD * VOX, CH)
    w = weight.reshape(TAPS * CH, CH)
    flipped = jnp.swapaxes(weight[::-1], 1, 2).reshape(TAPS * CH, CH)

    vox = vmem((16, 4, BP, CH), BF)
    slot_shape = vmem((SLOTS * 16, CH), BF)
    face_shape = vmem((16, BP, CH), BF)
    x_major, slots = pl.pallas_call(
        pack_kernel,
        out_shape=(vmem((VOX, BP, CH), BF), slot_shape),
        in_specs=[IN_VMEM, IN_SMEM],
        out_specs=(IN_VMEM, IN_VMEM),
        scratch_shapes=[pltpu.VMEM((BP * VOX, CH), F32), pltpu.VMEM((4, BP * 16, CH), F32)],
        compiler_params=params(),
        name="pack_features",
    )(feat, send_slot)
    x_major = x_major.reshape(16, 4, BP, CH)

    dma = pltpu.SemaphoreType.DMA
    recv, low, high = pl.pallas_call(
        first_exchange,
        out_shape=(slot_shape, face_shape, face_shape),
        in_specs=[IN_VMEM] * 2,
        out_specs=(IN_VMEM,) * 3,
        scratch_shapes=[dma, dma, dma((2,)), dma((2,))],
        compiler_params=params(collective_id=0, has_side_effects=True),
        name="exchange_features",
    )(slots, x_major)

    output, g_major, g_slots, grad = pl.pallas_call(
        forward_kernel,
        out_shape=(vmem((BD * VOX, CH), BF), vox, slot_shape, vmem((TPAD, CH, CH), F32)),
        in_specs=[IN_VMEM] * 4 + [IN_SMEM] * 2 + [IN_VMEM] * 5,
        out_specs=(IN_VMEM,) * 4,
        scratch_shapes=[
            pltpu.VMEM((6, 6, 6, BP, CH), BF),
            pltpu.VMEM((4, BP * 16, CH), F32),
            pltpu.VMEM((BP * VOX, CH), F32),
            pltpu.VMEM((BP * VOX, CH), F32),
            pltpu.VMEM((CH, BP * VOX), BF),
        ],
        compiler_params=params(),
        name="forward",
    )(x_major, recv, low, high, recv_slot, send_slot, lkeep, hkeep, w, cot, occ)

    recv2, low2, high2, total = pl.pallas_call(
        second_exchange,
        out_shape=(slot_shape, face_shape, face_shape, vmem((TPAD, CH, CH), F32)),
        in_specs=[IN_VMEM] * 3,
        out_specs=(IN_VMEM,) * 4,
        scratch_shapes=[
            pltpu.VMEM((HALF_T, CH, CH), F32),
            pltpu.VMEM((HALF_T, 8, CH), F32),
            pltpu.VMEM((HALF_T, 8, CH), F32),
            pltpu.VMEM((HALF_T, CH, CH), F32),
            pltpu.VMEM((NXY, HALF_T, 8, CH), F32),
            pltpu.VMEM((NZ, 8, CH), F32),
            dma, dma, dma((2,)), dma((2,)),
        ] + [dma((2,))] * 6,
        compiler_params=params(collective_id=1, has_side_effects=True),
        name="exchange_gradients",
    )(g_slots, g_major, grad)

    input_grad = pl.pallas_call(
        backward_kernel,
        out_shape=vmem((BD * VOX, CH), BF),
        in_specs=[IN_VMEM] * 4 + [IN_SMEM] + [IN_VMEM] * 4,
        out_specs=IN_VMEM,
        scratch_shapes=[
            pltpu.VMEM((6, 6, 6, BP, CH), BF),
            pltpu.VMEM((4, BP * 16, CH), F32),
            pltpu.VMEM((BP * VOX, CH), F32),
            pltpu.VMEM((BP * VOX, CH), F32),
        ],
        compiler_params=params(),
        name="backward",
    )(g_major, recv2, low2, high2, recv_slot, lkeep, hkeep, flipped, cot)

    weight_grad = total[:TAPS] * (BD * REG * SLB * float(VOX)) ** -0.5
    return output.reshape(features.shape), input_grad.reshape(features.shape), weight_grad


def solution(mesh):
    return jax.shard_map(
        shards,
        mesh=mesh,
        in_specs=(
            P(("region", "slab"), None, None, None, None),
            P(),
            P(("region", "slab"), None, None, None, None),
            P(("region", "slab"), None),
            P(("region", "slab"), None),
        ),
        out_specs=(
            P(("region", "slab"), None, None, None, None),
            P(("region", "slab"), None, None, None, None),
            P(),
        ),
        check_vma=False,
    )
```

```python
import functools

import jax
import jax.numpy as jnp
from jax import lax
from jax.experimental import pallas as pl
from jax.experimental.pallas import tpu as pltpu
from jax.sharding import PartitionSpec as P

MESH = pl.DeviceIdType.MESH
BF = jnp.bfloat16
F32 = jnp.float32

CH = 128
BD = 26
BP = 32
VOX = 64
REG = 128
SLB = 4
NX, NZ, NCORE = 4, 16, 2
NXY = NX * SLB
SLOTS = 2 * REG
TAPS = 27
HALF_T = 14
TPAD = 2 * HALF_T
CUTS = (1, 50, 70, 80, 90, REG)
VMEM_LIMIT = 50 * 1024 * 1024


def params(**kw):
    return pltpu.CompilerParams(vmem_limit_bytes=VMEM_LIMIT, **kw)


def vmem(shape, dtype):
    return jax.ShapeDtypeStruct(shape, dtype)


IN_VMEM = pl.BlockSpec(memory_space=pltpu.VMEM)
IN_SMEM = pl.BlockSpec(memory_space=pltpu.SMEM)
IN_ANY = pl.BlockSpec(memory_space=pl.ANY)


def face_voxels(side):
    if side == 0:
        return [4 * a + b for a in range(4) for b in range(4)]
    if side == 1:
        return [48 + 4 * a + b for a in range(4) for b in range(4)]
    if side == 2:
        return [16 * a + b for a in range(4) for b in range(4)]
    return [16 * a + 12 + b for a in range(4) for b in range(4)]


def fill_faces(slabs, faces):
    faces = faces.reshape(4, BP * 16, CH)
    for side in range(4):
        for t, v in enumerate(face_voxels(side)):
            faces[side, pl.ds(t, BP, stride=16), :] = slabs(v)


def zero_rim(pad):
    for a in (0, 5):
        for b in (0, 5):
            for c in range(6):
                pad[a, b, c] = jnp.zeros((BP, CH), BF)
                if 0 < c < 5:
                    pad[a, c, b] = jnp.zeros((BP, CH), BF)
                    pad[c, a, b] = jnp.zeros((BP, CH), BF)


def build_halo(pad, recv, slot_ref, low, high, lkeep, hkeep, faces):
    for i in range(4):
        for j in range(4):
            pad[i + 1, j + 1, 0] = (low[i, j].astype(F32) * lkeep[...]).astype(BF)
            pad[i + 1, j + 1, 5] = (high[i, j].astype(F32) * hkeep[...]).astype(BF)
    for side in range(4):

        def body(b, carry):
            faces[side * BP + b] = recv[slot_ref[side * BP + b]].astype(F32)
            return carry

        lax.fori_loop(0, BP, body, 0)
    faces = faces.reshape(4, BP * 16, CH)
    for side in range(4):
        for a in range(4):
            for b in range(4):
                slab = faces[side, pl.ds(4 * a + b, BP, stride=16), :].astype(BF)
                if side < 2:
                    pad[5 * side, a + 1, b + 1] = slab
                else:
                    pad[a + 1, 5 * (side - 2), b + 1] = slab


def conv_plane(pad, w_ref, plane):
    acc = None
    for o1 in range(3):
        for o2 in range(3):
            lhs = jnp.concatenate(
                [pad[plane + o1, o2 : o2 + 4, o3 : o3 + 4].reshape(16 * BP, CH) for o3 in range(3)],
                axis=1)
            tap = 9 * o1 + 3 * o2
            term = jnp.dot(lhs, w_ref[tap * CH : (tap + 3) * CH, :], preferred_element_type=F32)
            acc = term if acc is None else acc + term
    return acc


def place(axis_region, slab):
    core = lax.rem(axis_region, NCORE)
    z = lax.rem(axis_region // NCORE, NZ)
    x = axis_region // (NZ * NCORE)
    return x, z, core, x * SLB + slab


def pack_and_send(me, slab, lo, hi, faces, source_ref, slots, recv, send_sem, recv_sem):
    def send(k, carry):
        peer = lax.rem(me + k, REG)
        for half in range(2):
            source = source_ref[2 * peer + half]
            slots[2 * peer + half] = faces[source].astype(BF)
        pltpu.make_async_remote_copy(
            slots.at[pl.ds(2 * peer, 2)],
            recv.at[pl.ds(2 * me, 2)],
            send_sem, recv_sem,
            device_id={"region": peer, "slab": slab}, device_id_type=MESH,
        ).start()
        return carry

    lax.fori_loop(lo, hi, send, 0)


def slab_copies(me, slab, pad, low, high, z_send, z_recv):
    up = lax.rem(slab + 1, SLB)
    down = lax.rem(slab + SLB - 1, SLB)
    to_up = pltpu.make_async_remote_copy(
        pad.at[1:5, 1:5, 4], low, z_send.at[0], z_recv.at[0],
        device_id={"region": me, "slab": up}, device_id_type=MESH)
    to_down = pltpu.make_async_remote_copy(
        pad.at[1:5, 1:5, 1], high, z_send.at[1], z_recv.at[1],
        device_id={"region": me, "slab": down}, device_id_type=MESH)
    return to_up, to_down


def wait_bytes(ref, sem):
    pltpu.make_async_copy(ref, ref, sem).wait()


def section_kernel(feat, cot, w_ref, occ, lkeep, hkeep, source_ref, recv_slot,
                   out, input_grad, total,
                   padf, padg, wflip, rows, crows, outs, faces, slots, slots2, recv, recv2,
                   low, high, low2, high2, gt, grad,
                   part, col, mine, half_bf, all_bf, got0, got1, got2,
                   s1, r1, zs1, zr1, s2, r2, zs2, zr2, a_sem, b_sem, c_sem, d_sem, e_sem, f_sem):
    me = lax.axis_index("region")
    slab = lax.axis_index("slab")
    x, z, core, q = place(me, slab)

    def region_of(xx, zz, cc):
        return (xx * NZ + zz) * NCORE + cc

    def xy_peer(k):
        other = lax.rem(q + k, NXY)
        return other, {"region": region_of(other // SLB, z, core), "slab": lax.rem(other, SLB)}

    def z_peer(k):
        other = lax.rem(z + k, NZ)
        return other, {"region": region_of(x, other, core), "slab": slab}

    partner = {"region": region_of(x, z, 1 - core), "slab": slab}

    barrier = pltpu.get_barrier_semaphore()

    def greet(k, carry):
        pl.semaphore_signal(
            barrier, inc=1, device_id={"region": lax.rem(me + k, REG), "slab": slab},
            device_id_type=MESH)
        return carry

    lax.fori_loop(1, REG, greet, 0)

    def greet_slabs(k, carry):
        s = lax.rem(slab + 1 + lax.rem(k, SLB - 1), SLB)
        pl.semaphore_signal(
            barrier, inc=1, device_id={"region": region_of(k // (SLB - 1), z, core), "slab": s},
            device_id_type=MESH)
        return carry

    lax.fori_loop(0, NX * (SLB - 1), greet_slabs, 0)

    rows[0 : BD * VOX, :] = feat[...].astype(F32)
    rows[BD * VOX :, :] = jnp.zeros((BP * VOX - BD * VOX, CH), F32)
    for v in range(VOX):
        padf[v // 16 + 1, v // 4 % 4 + 1, v % 4 + 1] = rows[pl.ds(v, BP, stride=VOX), :].astype(BF)
    fill_faces(lambda v: rows[pl.ds(v, BP, stride=VOX), :], faces)

    pl.semaphore_wait(barrier, REG - 1 + NX * (SLB - 1))
    pair = slab_copies(me, slab, padf, low, high, zs1, zr1)
    for copy in pair:
        copy.start()
    pack_and_send(me, slab, 1, REG, faces, source_ref, slots, recv, s1, r1)

    zero_rim(padf)
    zero_rim(padg)
    for t in range(TAPS):
        wflip[t * CH : (t + 1) * CH, :] = w_ref[(TAPS - 1 - t) * CH : (TAPS - t) * CH, :].T
    crows[0 : BD * VOX, :] = cot[...].astype(F32)
    crows[BD * VOX :, :] = jnp.zeros((BP * VOX - BD * VOX, CH), F32)
    for t in range(TAPS, TPAD):
        grad[t] = jnp.zeros((CH, CH), F32)
    for buffer in (recv, recv2):
        for half in range(2):
            buffer[2 * me + half] = jnp.zeros((16, CH), BF)

    for copy in pair:
        copy.wait()
    peers = pl.ds(0, 2 * (REG - 1))
    wait_bytes(recv.at[peers], r1)
    wait_bytes(slots.at[peers], s1)

    build_halo(padf, recv, recv_slot, low, high, lkeep, hkeep, faces)

    def plane_body(plane, carry):
        pre = conv_plane(padf, w_ref, plane)
        mask = occ[plane]
        for t in range(16):
            u = pre[t * BP : (t + 1) * BP, :]
            s = 1.0 / (1.0 + jnp.exp(-u))
            m = mask[:, t : t + 1]
            f = padf[plane + 1, t // 4 + 1, t % 4 + 1].astype(F32)
            c = crows[pl.ds(16 * plane + t, BP, stride=VOX), :]
            outs[pl.ds(16 * plane + t, BP, stride=VOX), :] = f + m * (u * s)
            padg[plane + 1, t // 4 + 1, t % 4 + 1] = (c * m * s * (1.0 + u * (1.0 - s))).astype(BF)
        return carry

    lax.fori_loop(0, 4, plane_body, 0)
    fill_faces(lambda v: padg[v // 16 + 1, v // 4 % 4 + 1, v % 4 + 1].astype(F32), faces)
    pair = slab_copies(me, slab, padg, low2, high2, zs2, zr2)
    for copy in pair:
        copy.start()

    def send_faces(n):
        pack_and_send(me, slab, CUTS[n], CUTS[n + 1], faces, source_ref, slots2, recv2, s2, r2)

    send_faces(0)

    for i in range(4):
        for j in range(4):
            gt[:, 128 * (4 * i + j) : 128 * (4 * i + j + 1)] = (
                padg[i + 1, j + 1, 1:5].reshape(4 * BP, CH).T)

    def tap_body(n, carry):
        o1 = n // 3
        o2 = lax.rem(n, 3)
        rhs = jnp.concatenate(
            [padf[pl.ds(o1, 4), pl.ds(o2, 4), o3 : o3 + 4].reshape(VOX * BP, CH) for o3 in range(3)],
            axis=1)
        res = jnp.dot(gt[...], rhs, preferred_element_type=F32)
        for o3 in range(3):
            grad[3 * n + o3] = res[:, CH * o3 : CH * (o3 + 1)].T
        return carry

    lax.fori_loop(0, 9, tap_body, 0)

    own = pl.ds(core * HALF_T, HALF_T)
    other_half = pl.ds((1 - core) * HALF_T, HALF_T)
    pair0 = pltpu.make_async_remote_copy(
        grad.at[other_half], got0, a_sem.at[0], a_sem.at[1], device_id=partner, device_id_type=MESH)
    pair0.start()
    out[...] = outs[0 : BD * VOX, :].astype(BF)
    pair0.wait()

    def add_pair(t, carry):
        part[t] = grad[core * HALF_T + t] + got0[t]
        return carry

    lax.fori_loop(0, HALF_T, add_pair, 0)

    def send1(k, carry):
        other, device = xy_peer(k)
        pltpu.make_async_remote_copy(
            part.at[:, pl.ds(pl.multiple_of(other * 8, 8), 8)], got1.at[q],
            b_sem.at[0], b_sem.at[1], device_id=device, device_id_type=MESH).start()
        return carry

    lax.fori_loop(1, NXY, send1, 0)
    send_faces(1)
    got1[q] = part[:, pl.ds(pl.multiple_of(q * 8, 8), 8), :]
    span1 = got1.at[pl.ds(0, NXY - 1)]
    wait_bytes(span1, b_sem.at[1])
    wait_bytes(span1, b_sem.at[0])
    acc = got1[0]
    for k in range(1, NXY):
        acc = acc + got1[k]
    col[...] = acc

    def send2(k, carry):
        other, device = z_peer(k)

        @pl.when(other < HALF_T)
        def _():
            pltpu.make_async_remote_copy(
                col.at[other], got2.at[z],
                c_sem.at[0], c_sem.at[1], device_id=device, device_id_type=MESH).start()

        return carry

    lax.fori_loop(1, NZ, send2, 0)
    send_faces(2)

    @pl.when(z < HALF_T)
    def _():
        got2[z] = col[z]
        wait_bytes(got2.at[pl.ds(0, NZ - 1)], c_sem.at[1])
        wait_bytes(got2.at[pl.ds(0, HALF_T - 1)], c_sem.at[0])
        acc = got2[0]
        for k in range(1, NZ):
            acc = acc + got2[k]
        mine[z] = acc

    @pl.when(z >= HALF_T)
    def _():
        wait_bytes(got2.at[pl.ds(0, HALF_T)], c_sem.at[0])

    @pl.when(z < HALF_T)
    def _():
        def send3(k, carry):
            _, device = z_peer(k)
            pltpu.make_async_remote_copy(
                mine.at[z], mine.at[z],
                d_sem.at[0], d_sem.at[1], device_id=device, device_id_type=MESH).start()
            return carry

        lax.fori_loop(1, NZ, send3, 0)

    send_faces(3)

    @pl.when(z < HALF_T)
    def _():
        wait_bytes(mine.at[pl.ds(0, HALF_T - 1)], d_sem.at[1])
        wait_bytes(got2.at[pl.ds(0, NZ - 1)], d_sem.at[0])

    @pl.when(z >= HALF_T)
    def _():
        wait_bytes(mine.at[pl.ds(0, HALF_T)], d_sem.at[1])

    half_bf[...] = mine[...].reshape(HALF_T * 8, CH).astype(BF)

    def send4(k, carry):
        _, device = xy_peer(k)
        pltpu.make_async_remote_copy(
            half_bf, all_bf.at[core, q],
            e_sem.at[0], e_sem.at[1], device_id=device, device_id_type=MESH).start()
        return carry

    lax.fori_loop(1, NXY, send4, 0)
    send_faces(4)
    all_bf[core, q] = half_bf[...]
    span4 = all_bf.at[0, pl.ds(0, NXY - 1)]
    wait_bytes(span4, e_sem.at[1])
    wait_bytes(span4, e_sem.at[0])

    pair1 = pltpu.make_async_remote_copy(
        all_bf.at[core], all_bf.at[core], f_sem.at[0], f_sem.at[1], device_id=partner, device_id_type=MESH)
    pair1.start()
    pair1.wait()
    for c in range(NCORE):
        for k in range(NXY):
            total[HALF_T * c : HALF_T * (c + 1), 8 * k : 8 * k + 8, :] = (
                all_bf[c, k].astype(F32).reshape(HALF_T, 8, CH))

    for copy in pair:
        copy.wait()
    wait_bytes(recv2.at[peers], r2)
    wait_bytes(slots2.at[peers], s2)
    build_halo(padg, recv2, recv_slot, low2, high2, lkeep, hkeep, faces)

    def back_body(plane, carry):
        back = conv_plane(padg, wflip, plane)
        for t in range(16):
            c = crows[pl.ds(16 * plane + t, BP, stride=VOX), :]
            outs[pl.ds(16 * plane + t, BP, stride=VOX), :] = c + back[t * BP : (t + 1) * BP, :]
        return carry

    lax.fori_loop(0, 4, back_body, 0)
    input_grad[...] = outs[0 : BD * VOX, :].astype(BF)


def slot_tables(neighbors, me):
    linked = neighbors.T[:4].reshape(4 * BD)
    present = linked >= 0
    owner = jnp.where(present, linked // (BD * SLB), -1)
    position = linked % BD
    key = jnp.arange(4 * BD, dtype=jnp.int32)
    side = key // BD
    wanted = (side + 1 - 2 * (side % 2)) * BD + position
    same = owner[:, None] == owner[None, :]
    send_rank = jnp.sum(same & (key[None, :] < key[:, None]), axis=1, dtype=jnp.int32)
    recv_rank = jnp.sum(same & (wanted[None, :] < wanted[:, None]), axis=1, dtype=jnp.int32)
    send_slot = jnp.where(present, owner * 2 + send_rank, -1)
    recv_slot = jnp.where(present, owner * 2 + recv_rank, 2 * me)
    recv_slot = jnp.pad(recv_slot.reshape(4, BD), ((0, 0), (0, BP - BD)), constant_values=0)
    recv_slot = jnp.where(jnp.arange(BP)[None, :] < BD, recv_slot, 2 * me).reshape(4 * BP)
    slot = jnp.arange(SLOTS, dtype=jnp.int32)
    face = side * BP + key - side * BD
    source = jnp.sum(jnp.where(send_slot[None, :] == slot[:, None], face[None, :], 0), axis=1, dtype=jnp.int32)
    return source, recv_slot


def shards(features, weight, cotangent, occupancy, neighbors):
    source, recv_slot = slot_tables(neighbors, lax.axis_index("region"))
    keep = (neighbors[:, 4:6] >= 0).astype(F32)
    keep = jnp.pad(keep, ((0, BP - BD), (0, 0)))
    lkeep, hkeep = keep[:, 0:1], keep[:, 1:2]
    occ = jnp.pad(occupancy.astype(F32), ((0, BP - BD), (0, 0))).reshape(BP, 4, 16).swapaxes(0, 1)
    feat = features.reshape(BD * VOX, CH)
    cot = cotangent.reshape(BD * VOX, CH)
    w = weight.reshape(TAPS * CH, CH)

    dma = pltpu.SemaphoreType.DMA
    brick_rows = pltpu.VMEM((BP * VOX, CH), F32)
    pad_shape = pltpu.VMEM((6, 6, 6, BP, CH), BF)
    slot_shape = pltpu.VMEM((SLOTS, 16, CH), BF)
    plane_shape = pltpu.VMEM((4, 4, BP, CH), BF)
    half_shape = pltpu.VMEM((HALF_T, CH, CH), F32)
    tile_shape = pltpu.VMEM((HALF_T, 8, CH), F32)
    output, input_grad, total = pl.pallas_call(
        section_kernel,
        out_shape=(vmem((BD * VOX, CH), BF), vmem((BD * VOX, CH), BF), vmem((TPAD, CH, CH), F32)),
        in_specs=[IN_VMEM] * 6 + [IN_SMEM] * 2,
        out_specs=(IN_VMEM,) * 3,
        scratch_shapes=[
            pad_shape, pad_shape, pltpu.VMEM((TAPS * CH, CH), BF),
            brick_rows, brick_rows, brick_rows,
            pltpu.VMEM((4 * BP, 16, CH), F32),
            slot_shape, slot_shape, slot_shape, slot_shape,
            plane_shape, plane_shape, plane_shape, plane_shape,
            pltpu.VMEM((CH, BP * VOX), BF),
            pltpu.VMEM((TPAD, CH, CH), F32),
            half_shape, tile_shape, tile_shape,
            pltpu.VMEM((HALF_T * 8, CH), BF),
            pltpu.VMEM((NCORE, NXY, HALF_T * 8, CH), BF),
            half_shape,
            pltpu.VMEM((NXY, HALF_T, 8, CH), F32),
            pltpu.VMEM((NZ, 8, CH), F32),
            dma, dma, dma((2,)), dma((2,)), dma, dma, dma((2,)), dma((2,)),
        ] + [dma((2,))] * 6,
        compiler_params=params(collective_id=0, has_side_effects=True),
        name="section",
    )(feat, cot, w, occ, lkeep, hkeep, source, recv_slot)

    weight_grad = total[:TAPS] * (BD * REG * SLB * float(VOX)) ** -0.5
    return output.reshape(features.shape), input_grad.reshape(features.shape), weight_grad


def solution(mesh):
    return jax.shard_map(
        shards,
        mesh=mesh,
        in_specs=(
            P(("region", "slab"), None, None, None, None),
            P(),
            P(("region", "slab"), None, None, None, None),
            P(("region", "slab"), None),
            P(("region", "slab"), None),
        ),
        out_specs=(
            P(("region", "slab"), None, None, None, None),
            P(("region", "slab"), None, None, None, None),
            P(),
        ),
        check_vma=False,
    )
```

```python
import functools

import jax
import jax.numpy as jnp
from jax import lax
from jax.experimental import pallas as pl
from jax.experimental.pallas import tpu as pltpu
from jax.sharding import PartitionSpec as P

MESH = pl.DeviceIdType.MESH
BF = jnp.bfloat16
F32 = jnp.float32

CH = 128
BD = 26
BP = 32
VOX = 64
REG = 128
SLB = 4
NX, NZ, NCORE = 4, 16, 2
NXY = NX * SLB
SLOTS = 2 * REG
TAPS = 27
HALF_T = 14
TPAD = 2 * HALF_T
CUTS = (1, 50, 70, 80, 90, REG)
VMEM_LIMIT = 63 * 1024 * 1024


def params(**kw):
    return pltpu.CompilerParams(vmem_limit_bytes=VMEM_LIMIT, **kw)


def vmem(shape, dtype):
    return jax.ShapeDtypeStruct(shape, dtype)


IN_VMEM = pl.BlockSpec(memory_space=pltpu.VMEM)
IN_SMEM = pl.BlockSpec(memory_space=pltpu.SMEM)
IN_HBM = pl.BlockSpec(memory_space=pltpu.HBM)


def face_voxels(side):
    if side == 0:
        return [4 * a + b for a in range(4) for b in range(4)]
    if side == 1:
        return [48 + 4 * a + b for a in range(4) for b in range(4)]
    if side == 2:
        return [16 * a + b for a in range(4) for b in range(4)]
    return [16 * a + 12 + b for a in range(4) for b in range(4)]


def fill_faces(slabs, faces):
    faces = faces.reshape(4, BP * 16, CH)
    for side in range(4):
        for t, v in enumerate(face_voxels(side)):
            faces[side, pl.ds(t, BP, stride=16), :] = slabs(v)


def zero_rim(pad):
    for a in (0, 5):
        for b in (0, 5):
            for c in range(6):
                pad[a, b, c] = jnp.zeros((BP, CH), BF)
                if 0 < c < 5:
                    pad[a, c, b] = jnp.zeros((BP, CH), BF)
                    pad[c, a, b] = jnp.zeros((BP, CH), BF)


def build_halo(pad, recv, slot_ref, low, high, near_rows, faces):
    kept = jnp.concatenate(
        [(near_rows[...] >= 0).astype(F32), jnp.zeros((CH - 8, CH), F32)], axis=0).T[0:BP]
    lkeep = jnp.broadcast_to(kept[:, 4:5], (BP, CH)) > 0
    hkeep = jnp.broadcast_to(kept[:, 5:6], (BP, CH)) > 0
    nothing = jnp.zeros((BP, CH), F32)
    for i in range(4):
        for j in range(4):
            pad[i + 1, j + 1, 0] = jnp.where(lkeep, low[i, j].astype(F32), nothing).astype(BF)
            pad[i + 1, j + 1, 5] = jnp.where(hkeep, high[i, j].astype(F32), nothing).astype(BF)
    for side in range(4):

        def body(b, carry):
            faces[side * BP + b] = recv[slot_ref[side * BP + b]].astype(F32)
            return carry

        lax.fori_loop(0, BP, body, 0)
    faces = faces.reshape(4, BP * 16, CH)
    for side in range(4):
        for a in range(4):
            for b in range(4):
                slab = faces[side, pl.ds(4 * a + b, BP, stride=16), :].astype(BF)
                if side < 2:
                    pad[5 * side, a + 1, b + 1] = slab
                else:
                    pad[a + 1, 5 * (side - 2), b + 1] = slab


def pair_taps(pairs, tap_of):
    for n in range(9):
        for c in range(4):
            for e in range(2):
                block = tap_of(3 * n + c - e) if 0 <= c - e <= 2 else jnp.zeros((CH, CH), BF)
                pairs[512 * n + CH * c : 512 * n + CH * (c + 1), CH * e : CH * (e + 1)] = block


def conv_plane(pad, pairs, plane):
    acc = None
    for o1 in range(3):
        halves = []
        for p in range(2):
            halves.append(jnp.concatenate(
                [pad[plane + o1, o2 : o2 + 4, 2 * p + c].reshape(4 * BP, CH) for o2 in range(3) for c in range(4)],
                axis=1))
        lhs = jnp.concatenate(halves, axis=0)
        term = jnp.dot(lhs, pairs[1536 * o1 : 1536 * (o1 + 1), :], preferred_element_type=F32)
        acc = term if acc is None else acc + term
    return acc


def voxel_rows(values, t):
    j, k = t // 4, t % 4
    row = (k // 2) * 4 * BP + j * BP
    return values[row : row + BP, (k % 2) * CH : (k % 2 + 1) * CH]


def place(axis_region, slab):
    core = lax.rem(axis_region, NCORE)
    z = lax.rem(axis_region // NCORE, NZ)
    x = axis_region // (NZ * NCORE)
    return x, z, core, x * SLB + slab


def pack_and_send(me, slab, lo, hi, faces, source_ref, slots, recv, send_sem, recv_sem):
    def send(k, carry):
        peer = lax.rem(me + k, REG)
        for half in range(2):
            source = source_ref[2 * peer + half]
            slots[2 * peer + half] = faces[source].astype(BF)
        pltpu.make_async_remote_copy(
            slots.at[pl.ds(2 * peer, 2)],
            recv.at[pl.ds(2 * me, 2)],
            send_sem, recv_sem,
            device_id={"region": peer, "slab": slab}, device_id_type=MESH,
        ).start()
        return carry

    lax.fori_loop(lo, hi, send, 0)


def slab_copies(me, slab, pad, low, high, z_send, z_recv):
    up = lax.rem(slab + 1, SLB)
    down = lax.rem(slab + SLB - 1, SLB)
    to_up = pltpu.make_async_remote_copy(
        pad.at[1:5, 1:5, 4], low, z_send.at[0], z_recv.at[0],
        device_id={"region": me, "slab": up}, device_id_type=MESH)
    to_down = pltpu.make_async_remote_copy(
        pad.at[1:5, 1:5, 1], high, z_send.at[1], z_recv.at[1],
        device_id={"region": me, "slab": down}, device_id_type=MESH)
    return to_up, to_down


def wait_bytes(ref, sem):
    pltpu.make_async_copy(ref, ref, sem).wait()


def section_kernel(feat_hbm, cot_hbm, w_hbm, occupancy, near, source_ref, recv_slot,
                   out, input_grad, total_bf,
                   feat, cot, w_ref, occ, total, near_rows, i_sem,
                   padf, padg, taps_f, taps_b, rows, crows, outs, faces, slots, slots2, recv, recv2,
                   low, high, low2, high2, gt, grad,
                   part, col, mine, half_bf, all_bf, got0, got1, got2,
                   s1, r1, zs1, zr1, s2, r2, zs2, zr2, a_sem, b_sem, c_sem, d_sem, e_sem, f_sem):
    me = lax.axis_index("region")
    slab = lax.axis_index("slab")
    x, z, core, q = place(me, slab)

    def region_of(xx, zz, cc):
        return (xx * NZ + zz) * NCORE + cc

    def xy_peer(k):
        other = lax.rem(q + k, NXY)
        return other, {"region": region_of(other // SLB, z, core), "slab": lax.rem(other, SLB)}

    def z_peer(k):
        other = lax.rem(z + k, NZ)
        return other, {"region": region_of(x, other, core), "slab": slab}

    partner = {"region": region_of(x, z, 1 - core), "slab": slab}

    fetch = [pltpu.make_async_copy(a, b, i_sem.at[n])
             for n, (a, b) in enumerate(((feat_hbm, feat), (cot_hbm, cot), (w_hbm, w_ref)))]
    fetch[0].start()

    barrier = pltpu.get_barrier_semaphore()

    def greet(k, carry):
        pl.semaphore_signal(
            barrier, inc=1, device_id={"region": lax.rem(me + k, REG), "slab": slab},
            device_id_type=MESH)
        return carry

    lax.fori_loop(1, REG, greet, 0)

    def greet_slabs(k, carry):
        s = lax.rem(slab + 1 + lax.rem(k, SLB - 1), SLB)
        pl.semaphore_signal(
            barrier, inc=1, device_id={"region": region_of(k // (SLB - 1), z, core), "slab": s},
            device_id_type=MESH)
        return carry

    lax.fori_loop(0, NX * (SLB - 1), greet_slabs, 0)

    near_rows[...] = jnp.full((8, CH), -1, jnp.int32)
    near_rows[0:6, 0:BD] = near[...]

    fetch[0].wait()
    rows[0 : BD * VOX, :] = feat[...].astype(F32)
    rows[BD * VOX :, :] = jnp.zeros((BP * VOX - BD * VOX, CH), F32)
    for v in range(VOX):
        padf[v // 16 + 1, v // 4 % 4 + 1, v % 4 + 1] = rows[pl.ds(v, BP, stride=VOX), :].astype(BF)
    fill_faces(lambda v: rows[pl.ds(v, BP, stride=VOX), :], faces)

    pl.semaphore_wait(barrier, REG - 1 + NX * (SLB - 1))
    pair = slab_copies(me, slab, padf, low, high, zs1, zr1)
    for copy in pair:
        copy.start()
    pack_and_send(me, slab, 1, REG, faces, source_ref, slots, recv, s1, r1)

    fetch[2].start()
    fetch[1].start()
    for p in range(4):
        occ[p] = jnp.zeros((BP, 16), F32)
        occ[p, 0:BD, :] = occupancy[:, 16 * p : 16 * p + 16].astype(F32)
    zero_rim(padf)
    zero_rim(padg)
    fetch[2].wait()
    pair_taps(taps_f, lambda t: w_ref[t * CH : (t + 1) * CH, :])
    pair_taps(taps_b, lambda t: w_ref[(TAPS - 1 - t) * CH : (TAPS - t) * CH, :].T)
    fetch[1].wait()
    crows[0 : BD * VOX, :] = cot[...].astype(F32)
    crows[BD * VOX :, :] = jnp.zeros((BP * VOX - BD * VOX, CH), F32)
    for t in range(TAPS, TPAD):
        grad[t] = jnp.zeros((CH, CH), F32)
    for buffer in (recv, recv2):
        for half in range(2):
            buffer[2 * me + half] = jnp.zeros((16, CH), BF)

    for copy in pair:
        copy.wait()
    peers = pl.ds(0, 2 * (REG - 1))
    wait_bytes(recv.at[peers], r1)
    wait_bytes(slots.at[peers], s1)

    build_halo(padf, recv, recv_slot, low, high, near_rows, faces)

    def plane_body(plane, carry):
        pre = conv_plane(padf, taps_f, plane)
        mask = occ[plane]
        for t in range(16):
            u = voxel_rows(pre, t)
            s = 1.0 / (1.0 + jnp.exp(-u))
            m = mask[:, t : t + 1]
            f = padf[plane + 1, t // 4 + 1, t % 4 + 1].astype(F32)
            c = crows[pl.ds(16 * plane + t, BP, stride=VOX), :]
            outs[pl.ds(16 * plane + t, BP, stride=VOX), :] = f + m * (u * s)
            padg[plane + 1, t // 4 + 1, t % 4 + 1] = (c * m * s * (1.0 + u * (1.0 - s))).astype(BF)
        return carry

    lax.fori_loop(0, 4, plane_body, 0)
    fill_faces(lambda v: padg[v // 16 + 1, v // 4 % 4 + 1, v % 4 + 1].astype(F32), faces)
    pair = slab_copies(me, slab, padg, low2, high2, zs2, zr2)
    for copy in pair:
        copy.start()

    def send_faces(n):
        pack_and_send(me, slab, CUTS[n], CUTS[n + 1], faces, source_ref, slots2, recv2, s2, r2)

    send_faces(0)

    for i in range(4):
        for j in range(4):
            gt[:, 128 * (4 * i + j) : 128 * (4 * i + j + 1)] = (
                padg[i + 1, j + 1, 1:5].reshape(4 * BP, CH).T)

    def tap_body(n, carry):
        o1 = n // 3
        o2 = lax.rem(n, 3)
        rhs = jnp.concatenate(
            [padf[pl.ds(o1, 4), pl.ds(o2, 4), o3 : o3 + 4].reshape(VOX * BP, CH) for o3 in range(3)],
            axis=1)
        res = jnp.dot(gt[...], rhs, preferred_element_type=F32)
        for o3 in range(3):
            grad[3 * n + o3] = res[:, CH * o3 : CH * (o3 + 1)].T
        return carry

    lax.fori_loop(0, 9, tap_body, 0)

    def back_plane(plane):
        back = conv_plane(padg, taps_b, plane)
        for t in range(16):
            c = crows[pl.ds(16 * plane + t, BP, stride=VOX), :]
            outs[pl.ds(16 * plane + t, BP, stride=VOX), :] = c + voxel_rows(back, t)

    own = pl.ds(core * HALF_T, HALF_T)
    other_half = pl.ds((1 - core) * HALF_T, HALF_T)
    pair0 = pltpu.make_async_remote_copy(
        grad.at[other_half], got0, a_sem.at[0], a_sem.at[1], device_id=partner, device_id_type=MESH)
    pair0.start()
    out[...] = outs[0 : BD * VOX, :].astype(BF)
    pair0.wait()

    def add_pair(t, carry):
        part[t] = grad[core * HALF_T + t] + got0[t]
        return carry

    lax.fori_loop(0, HALF_T, add_pair, 0)

    def send1(k, carry):
        other, device = xy_peer(k)
        pltpu.make_async_remote_copy(
            part.at[:, pl.ds(pl.multiple_of(other * 8, 8), 8)], got1.at[q],
            b_sem.at[0], b_sem.at[1], device_id=device, device_id_type=MESH).start()
        return carry

    lax.fori_loop(1, NXY, send1, 0)
    send_faces(1)
    got1[q] = part[:, pl.ds(pl.multiple_of(q * 8, 8), 8), :]
    span1 = got1.at[pl.ds(0, NXY - 1)]
    wait_bytes(span1, b_sem.at[1])
    wait_bytes(span1, b_sem.at[0])
    acc = got1[0]
    for k in range(1, NXY):
        acc = acc + got1[k]
    col[...] = acc

    def send2(k, carry):
        other, device = z_peer(k)

        @pl.when(other < HALF_T)
        def _():
            pltpu.make_async_remote_copy(
                col.at[other], got2.at[z],
                c_sem.at[0], c_sem.at[1], device_id=device, device_id_type=MESH).start()

        return carry

    lax.fori_loop(1, NZ, send2, 0)
    send_faces(2)

    @pl.when(z < HALF_T)
    def _():
        got2[z] = col[z]
        wait_bytes(got2.at[pl.ds(0, NZ - 1)], c_sem.at[1])
        wait_bytes(got2.at[pl.ds(0, HALF_T - 1)], c_sem.at[0])
        acc = got2[0]
        for k in range(1, NZ):
            acc = acc + got2[k]
        mine[z] = acc

    @pl.when(z >= HALF_T)
    def _():
        wait_bytes(got2.at[pl.ds(0, HALF_T)], c_sem.at[0])

    @pl.when(z < HALF_T)
    def _():
        def send3(k, carry):
            _, device = z_peer(k)
            pltpu.make_async_remote_copy(
                mine.at[z], mine.at[z],
                d_sem.at[0], d_sem.at[1], device_id=device, device_id_type=MESH).start()
            return carry

        lax.fori_loop(1, NZ, send3, 0)

    send_faces(3)

    @pl.when(z < HALF_T)
    def _():
        wait_bytes(mine.at[pl.ds(0, HALF_T - 1)], d_sem.at[1])
        wait_bytes(got2.at[pl.ds(0, NZ - 1)], d_sem.at[0])

    @pl.when(z >= HALF_T)
    def _():
        wait_bytes(mine.at[pl.ds(0, HALF_T)], d_sem.at[1])

    half_bf[...] = mine[...].reshape(HALF_T * 8, CH).astype(BF)

    def send4(k, carry):
        _, device = xy_peer(k)
        pltpu.make_async_remote_copy(
            half_bf, all_bf.at[core, q],
            e_sem.at[0], e_sem.at[1], device_id=device, device_id_type=MESH).start()
        return carry

    lax.fori_loop(1, NXY, send4, 0)
    send_faces(4)
    all_bf[core, q] = half_bf[...]

    for copy in pair:
        copy.wait()
    wait_bytes(recv2.at[peers], r2)
    build_halo(padg, recv2, recv_slot, low2, high2, near_rows, faces)
    back_plane(0)
    back_plane(1)
    back_plane(2)
    back_plane(3)
    span4 = all_bf.at[0, pl.ds(0, NXY - 1)]
    wait_bytes(span4, e_sem.at[1])
    wait_bytes(span4, e_sem.at[0])

    pair1 = pltpu.make_async_remote_copy(
        all_bf.at[core], all_bf.at[core], f_sem.at[0], f_sem.at[1], device_id=partner, device_id_type=MESH)
    pair1.start()
    input_grad[...] = outs[0 : BD * VOX, :].astype(BF)
    wait_bytes(slots2.at[peers], s2)
    pair1.wait()
    for c in range(NCORE):
        for k in range(NXY):
            total[HALF_T * c : HALF_T * (c + 1), 8 * k : 8 * k + 8, :] = (
                all_bf[c, k].astype(F32).reshape(HALF_T, 8, CH))
    total_bf[...] = total[0:TAPS].astype(BF)

def slot_tables(neighbors, me):
    linked = neighbors.T[:4].reshape(4 * BD)
    present = linked >= 0
    owner = jnp.where(present, linked // (BD * SLB), -1)
    position = linked % BD
    key = jnp.arange(4 * BD, dtype=jnp.int32)
    side = key // BD
    wanted = (side + 1 - 2 * (side % 2)) * BD + position
    same = owner[:, None] == owner[None, :]
    send_rank = jnp.sum(same & (key[None, :] < key[:, None]), axis=1, dtype=jnp.int32)
    recv_rank = jnp.sum(same & (wanted[None, :] < wanted[:, None]), axis=1, dtype=jnp.int32)
    send_slot = jnp.where(present, owner * 2 + send_rank, -1)
    recv_slot = jnp.where(present, owner * 2 + recv_rank, 2 * me)
    recv_slot = jnp.pad(recv_slot.reshape(4, BD), ((0, 0), (0, BP - BD)), constant_values=0)
    recv_slot = jnp.where(jnp.arange(BP)[None, :] < BD, recv_slot, 2 * me).reshape(4 * BP)
    slot = jnp.arange(SLOTS, dtype=jnp.int32)
    face = side * BP + key - side * BD
    source = jnp.sum(jnp.where(send_slot[None, :] == slot[:, None], face[None, :], 0), axis=1, dtype=jnp.int32)
    return source, recv_slot


def shards(features, weight, cotangent, occupancy, neighbors):
    source, recv_slot = slot_tables(neighbors, lax.axis_index("region"))
    feat = features.reshape(BD * VOX, CH)
    cot = cotangent.reshape(BD * VOX, CH)
    w = weight.reshape(TAPS * CH, CH)

    dma = pltpu.SemaphoreType.DMA
    brick_rows = pltpu.VMEM((BP * VOX, CH), F32)
    pad_shape = pltpu.VMEM((6, 6, 6, BP, CH), BF)
    slot_shape = pltpu.VMEM((SLOTS, 16, CH), BF)
    plane_shape = pltpu.VMEM((4, 4, BP, CH), BF)
    half_shape = pltpu.VMEM((HALF_T, CH, CH), F32)
    tile_shape = pltpu.VMEM((HALF_T, 8, CH), F32)
    output, input_grad, total = pl.pallas_call(
        section_kernel,
        out_shape=(vmem((BD * VOX, CH), BF), vmem((BD * VOX, CH), BF), vmem((TAPS, CH, CH), BF)),
        in_specs=[IN_HBM] * 3 + [IN_VMEM] * 2 + [IN_SMEM] * 2,
        out_specs=(IN_VMEM,) * 3,
        scratch_shapes=[
            pltpu.VMEM((BD * VOX, CH), BF), pltpu.VMEM((BD * VOX, CH), BF), pltpu.VMEM((TAPS * CH, CH), BF),
            pltpu.VMEM((4, BP, 16), F32), pltpu.VMEM((TPAD, CH, CH), F32),
            pltpu.VMEM((8, CH), jnp.int32), dma((3,)),
            pad_shape, pad_shape, pltpu.VMEM((9 * 512, 256), BF), pltpu.VMEM((9 * 512, 256), BF),
            brick_rows, brick_rows, brick_rows,
            pltpu.VMEM((4 * BP, 16, CH), F32),
            slot_shape, slot_shape, slot_shape, slot_shape,
            plane_shape, plane_shape, plane_shape, plane_shape,
            pltpu.VMEM((CH, BP * VOX), BF),
            pltpu.VMEM((TPAD, CH, CH), F32),
            half_shape, tile_shape, tile_shape,
            pltpu.VMEM((HALF_T * 8, CH), BF),
            pltpu.VMEM((NCORE, NXY, HALF_T * 8, CH), BF),
            half_shape,
            pltpu.VMEM((NXY, HALF_T, 8, CH), F32),
            pltpu.VMEM((NZ, 8, CH), F32),
            dma, dma, dma((2,)), dma((2,)), dma, dma, dma((2,)), dma((2,)),
        ] + [dma((2,))] * 6,
        compiler_params=params(collective_id=0, has_side_effects=True),
        name="section",
    )(feat, cot, w, occupancy, neighbors.T, source, recv_slot)

    weight_grad = total.astype(F32) * (BD * REG * SLB * float(VOX)) ** -0.5
    return output.reshape(features.shape), input_grad.reshape(features.shape), weight_grad


def solution(mesh):
    return jax.shard_map(
        shards,
        mesh=mesh,
        in_specs=(
            P(("region", "slab"), None, None, None, None),
            P(),
            P(("region", "slab"), None, None, None, None),
            P(("region", "slab"), None),
            P(("region", "slab"), None),
        ),
        out_specs=(
            P(("region", "slab"), None, None, None, None),
            P(("region", "slab"), None, None, None, None),
            P(),
        ),
        check_vma=False,
    )
```

```python
import functools

import jax
import jax.numpy as jnp
from jax import lax
from jax.experimental import pallas as pl
from jax.experimental.pallas import tpu as pltpu
from jax.sharding import PartitionSpec as P

MESH = pl.DeviceIdType.MESH
BF = jnp.bfloat16
F32 = jnp.float32

CH = 128
BD = 26
BP = 32
VOX = 64
REG = 128
SLB = 4
NX, NZ, NCORE = 4, 16, 2
NXY = NX * SLB
SLOTS = 2 * REG
TAPS = 27
HALF_T = 14
TPAD = 2 * HALF_T
CUTS = (1, 50, 70, 80, 90, REG)
VMEM_LIMIT = 63 * 1024 * 1024


def params(**kw):
    return pltpu.CompilerParams(vmem_limit_bytes=VMEM_LIMIT, **kw)


def vmem(shape, dtype):
    return jax.ShapeDtypeStruct(shape, dtype)


IN_VMEM = pl.BlockSpec(memory_space=pltpu.VMEM)
IN_SMEM = pl.BlockSpec(memory_space=pltpu.SMEM)
IN_HBM = pl.BlockSpec(memory_space=pltpu.HBM)


def face_voxels(side):
    if side == 0:
        return [4 * a + b for a in range(4) for b in range(4)]
    if side == 1:
        return [48 + 4 * a + b for a in range(4) for b in range(4)]
    if side == 2:
        return [16 * a + b for a in range(4) for b in range(4)]
    return [16 * a + 12 + b for a in range(4) for b in range(4)]


def fill_faces(slabs, faces):
    faces = faces.reshape(4, BP * 16, CH)
    for side in range(4):
        for t, v in enumerate(face_voxels(side)):
            faces[side, pl.ds(t, BP, stride=16), :] = slabs(v)


def zero_rim(pad):
    for a in (0, 5):
        for b in (0, 5):
            for c in range(6):
                pad[a, b, c] = jnp.zeros((BP, CH), BF)
                if 0 < c < 5:
                    pad[a, c, b] = jnp.zeros((BP, CH), BF)
                    pad[c, a, b] = jnp.zeros((BP, CH), BF)


def build_halo(pad, recv, slot_ref, low, high, near_rows, faces):
    kept = jnp.concatenate(
        [(near_rows[...] >= 0).astype(F32), jnp.zeros((CH - 8, CH), F32)], axis=0).T[0:BP]
    lkeep = jnp.broadcast_to(kept[:, 4:5], (BP, CH)) > 0
    hkeep = jnp.broadcast_to(kept[:, 5:6], (BP, CH)) > 0
    nothing = jnp.zeros((BP, CH), F32)
    for i in range(4):
        for j in range(4):
            pad[i + 1, j + 1, 0] = jnp.where(lkeep, low[i, j].astype(F32), nothing).astype(BF)
            pad[i + 1, j + 1, 5] = jnp.where(hkeep, high[i, j].astype(F32), nothing).astype(BF)
    for side in range(4):

        def body(b, carry):
            faces[side * BP + b] = recv[slot_ref[side * BD + b]].astype(F32)
            return carry

        lax.fori_loop(0, BD, body, 0)
    faces = faces.reshape(4, BP * 16, CH)
    for side in range(4):
        for a in range(4):
            for b in range(4):
                slab = faces[side, pl.ds(4 * a + b, BP, stride=16), :].astype(BF)
                if side < 2:
                    pad[5 * side, a + 1, b + 1] = slab
                else:
                    pad[a + 1, 5 * (side - 2), b + 1] = slab


def pair_taps(pairs, tap_of):
    for n in range(9):
        for c in range(4):
            for e in range(2):
                block = tap_of(3 * n + c - e) if 0 <= c - e <= 2 else jnp.zeros((CH, CH), BF)
                pairs[512 * n + CH * c : 512 * n + CH * (c + 1), CH * e : CH * (e + 1)] = block


def conv_plane(pad, pairs, plane):
    acc = None
    for o1 in range(3):
        halves = []
        for p in range(2):
            halves.append(jnp.concatenate(
                [pad[plane + o1, o2 : o2 + 4, 2 * p + c].reshape(4 * BP, CH) for o2 in range(3) for c in range(4)],
                axis=1))
        lhs = jnp.concatenate(halves, axis=0)
        term = jnp.dot(lhs, pairs[1536 * o1 : 1536 * (o1 + 1), :], preferred_element_type=F32)
        acc = term if acc is None else acc + term
    return acc


def voxel_rows(values, t):
    j, k = t // 4, t % 4
    row = (k // 2) * 4 * BP + j * BP
    return values[row : row + BP, (k % 2) * CH : (k % 2 + 1) * CH]


def place(axis_region, slab):
    core = lax.rem(axis_region, NCORE)
    z = lax.rem(axis_region // NCORE, NZ)
    x = axis_region // (NZ * NCORE)
    return x, z, core, x * SLB + slab


def pack_and_send(me, slab, lo, hi, faces, source_ref, slots, recv, send_sem, recv_sem):
    def send(k, carry):
        peer = lax.rem(me + k, REG)
        for half in range(2):
            source = source_ref[2 * peer + half]
            slots[2 * peer + half] = faces[source].astype(BF)
        pltpu.make_async_remote_copy(
            slots.at[pl.ds(2 * peer, 2)],
            recv.at[pl.ds(2 * me, 2)],
            send_sem, recv_sem,
            device_id={"region": peer, "slab": slab}, device_id_type=MESH,
        ).start()
        return carry

    lax.fori_loop(lo, hi, send, 0)


def slab_copies(me, slab, pad, low, high, z_send, z_recv):
    up = lax.rem(slab + 1, SLB)
    down = lax.rem(slab + SLB - 1, SLB)
    to_up = pltpu.make_async_remote_copy(
        pad.at[1:5, 1:5, 4], low, z_send.at[0], z_recv.at[0],
        device_id={"region": me, "slab": up}, device_id_type=MESH)
    to_down = pltpu.make_async_remote_copy(
        pad.at[1:5, 1:5, 1], high, z_send.at[1], z_recv.at[1],
        device_id={"region": me, "slab": down}, device_id_type=MESH)
    return to_up, to_down


def wait_bytes(ref, sem):
    pltpu.make_async_copy(ref, ref, sem).wait()


def section_kernel(feat_hbm, cot_hbm, w_hbm, occupancy, near, source_ref, recv_slot,
                   out, input_grad, total_bf,
                   feat, cot, w_ref, occ, total, near_rows, i_sem,
                   padf, padg, taps_f, taps_b, rows, crows, outs, faces, slots, slots2, recv, recv2,
                   low, high, low2, high2, gt, grad,
                   part, col, mine, half_bf, all_bf, got0, got1, got2,
                   s1, r1, zs1, zr1, s2, r2, zs2, zr2, a_sem, b_sem, c_sem, d_sem, e_sem, f_sem):
    me = lax.axis_index("region")
    slab = lax.axis_index("slab")
    x, z, core, q = place(me, slab)

    def region_of(xx, zz, cc):
        return (xx * NZ + zz) * NCORE + cc

    def xy_peer(k):
        other = lax.rem(q + k, NXY)
        return other, {"region": region_of(other // SLB, z, core), "slab": lax.rem(other, SLB)}

    def z_peer(k):
        other = lax.rem(z + k, NZ)
        return other, {"region": region_of(x, other, core), "slab": slab}

    partner = {"region": region_of(x, z, 1 - core), "slab": slab}

    fetch = [pltpu.make_async_copy(a, b, i_sem.at[n])
             for n, (a, b) in enumerate(((feat_hbm, feat), (cot_hbm, cot), (w_hbm, w_ref)))]
    fetch[0].start()

    barrier = pltpu.get_barrier_semaphore()

    def greet(k, carry):
        pl.semaphore_signal(
            barrier, inc=1, device_id={"region": lax.rem(me + k, REG), "slab": slab},
            device_id_type=MESH)
        return carry

    lax.fori_loop(1, REG, greet, 0)

    def greet_slabs(k, carry):
        s = lax.rem(slab + 1 + lax.rem(k, SLB - 1), SLB)
        pl.semaphore_signal(
            barrier, inc=1, device_id={"region": region_of(k // (SLB - 1), z, core), "slab": s},
            device_id_type=MESH)
        return carry

    lax.fori_loop(0, NX * (SLB - 1), greet_slabs, 0)

    near_rows[...] = jnp.full((8, CH), -1, jnp.int32)
    near_rows[0:6, 0:BD] = near[...]

    fetch[0].wait()
    rows[0 : BD * VOX, :] = feat[...].astype(F32)
    rows[BD * VOX :, :] = jnp.zeros((BP * VOX - BD * VOX, CH), F32)
    for v in range(VOX):
        padf[v // 16 + 1, v // 4 % 4 + 1, v % 4 + 1] = rows[pl.ds(v, BP, stride=VOX), :].astype(BF)
    fill_faces(lambda v: rows[pl.ds(v, BP, stride=VOX), :], faces)

    pl.semaphore_wait(barrier, REG - 1 + NX * (SLB - 1))
    pair = slab_copies(me, slab, padf, low, high, zs1, zr1)
    for copy in pair:
        copy.start()
    pack_and_send(me, slab, 1, REG, faces, source_ref, slots, recv, s1, r1)

    fetch[2].start()
    fetch[1].start()
    for p in range(4):
        occ[p] = jnp.zeros((BP, 16), F32)
        occ[p, 0:BD, :] = occupancy[:, 16 * p : 16 * p + 16].astype(F32)
    zero_rim(padf)
    zero_rim(padg)
    fetch[2].wait()
    pair_taps(taps_f, lambda t: w_ref[t * CH : (t + 1) * CH, :])
    pair_taps(taps_b, lambda t: w_ref[(TAPS - 1 - t) * CH : (TAPS - t) * CH, :].T)
    fetch[1].wait()
    crows[0 : BD * VOX, :] = cot[...].astype(F32)
    crows[BD * VOX :, :] = jnp.zeros((BP * VOX - BD * VOX, CH), F32)
    for t in range(TAPS, TPAD):
        grad[t] = jnp.zeros((CH, CH), F32)
    for buffer in (recv, recv2):
        for half in range(2):
            buffer[2 * me + half] = jnp.zeros((16, CH), BF)

    for copy in pair:
        copy.wait()
    peers = pl.ds(0, 2 * (REG - 1))
    wait_bytes(recv.at[peers], r1)
    wait_bytes(slots.at[peers], s1)

    build_halo(padf, recv, recv_slot, low, high, near_rows, faces)

    def plane_body(plane, carry):
        pre = conv_plane(padf, taps_f, plane)
        mask = occ[plane]
        for t in range(16):
            u = voxel_rows(pre, t)
            s = 1.0 / (1.0 + jnp.exp(-u))
            m = mask[:, t : t + 1]
            f = padf[plane + 1, t // 4 + 1, t % 4 + 1].astype(F32)
            c = crows[pl.ds(16 * plane + t, BP, stride=VOX), :]
            outs[pl.ds(16 * plane + t, BP, stride=VOX), :] = f + m * (u * s)
            padg[plane + 1, t // 4 + 1, t % 4 + 1] = (c * m * s * (1.0 + u * (1.0 - s))).astype(BF)
        return carry

    lax.fori_loop(0, 4, plane_body, 0)
    fill_faces(lambda v: padg[v // 16 + 1, v // 4 % 4 + 1, v % 4 + 1].astype(F32), faces)
    pair = slab_copies(me, slab, padg, low2, high2, zs2, zr2)
    for copy in pair:
        copy.start()

    def send_faces(n):
        pack_and_send(me, slab, CUTS[n], CUTS[n + 1], faces, source_ref, slots2, recv2, s2, r2)

    send_faces(0)

    for i in range(4):
        for j in range(4):
            gt[:, 128 * (4 * i + j) : 128 * (4 * i + j + 1)] = (
                padg[i + 1, j + 1, 1:5].reshape(4 * BP, CH).T)

    def tap_body(n, carry):
        n = lax.rem(n + 4 * (1 - core), 9)
        o1 = n // 3
        o2 = lax.rem(n, 3)
        rhs = jnp.concatenate(
            [padf[pl.ds(o1, 4), pl.ds(o2, 4), o3 : o3 + 4].reshape(VOX * BP, CH) for o3 in range(3)],
            axis=1)
        res = jnp.dot(gt[...], rhs, preferred_element_type=F32)
        for o3 in range(3):
            grad[3 * n + o3] = res[:, CH * o3 : CH * (o3 + 1)].T
        return carry

    lax.fori_loop(0, 5, tap_body, 0)

    def back_plane(plane):
        back = conv_plane(padg, taps_b, plane)
        for t in range(16):
            c = crows[pl.ds(16 * plane + t, BP, stride=VOX), :]
            outs[pl.ds(16 * plane + t, BP, stride=VOX), :] = c + voxel_rows(back, t)

    own = pl.ds(core * HALF_T, HALF_T)
    other_half = pl.ds((1 - core) * HALF_T, HALF_T)
    pair0 = pltpu.make_async_remote_copy(
        grad.at[other_half], got0, a_sem.at[0], a_sem.at[1], device_id=partner, device_id_type=MESH)
    pair0.start()
    lax.fori_loop(5, 9, tap_body, 0)
    out[...] = outs[0 : BD * VOX, :].astype(BF)
    pair0.wait()

    def add_pair(t, carry):
        part[t] = grad[core * HALF_T + t] + got0[t]
        return carry

    lax.fori_loop(0, HALF_T, add_pair, 0)

    def send1(k, carry):
        other, device = xy_peer(k)
        pltpu.make_async_remote_copy(
            part.at[:, pl.ds(pl.multiple_of(other * 8, 8), 8)], got1.at[q],
            b_sem.at[0], b_sem.at[1], device_id=device, device_id_type=MESH).start()
        return carry

    lax.fori_loop(1, NXY, send1, 0)
    send_faces(1)
    got1[q] = part[:, pl.ds(pl.multiple_of(q * 8, 8), 8), :]
    span1 = got1.at[pl.ds(0, NXY - 1)]
    wait_bytes(span1, b_sem.at[1])
    wait_bytes(span1, b_sem.at[0])
    acc = got1[0]
    for k in range(1, NXY):
        acc = acc + got1[k]
    col[...] = acc

    def send2(k, carry):
        other, device = z_peer(k)

        @pl.when(other < HALF_T)
        def _():
            pltpu.make_async_remote_copy(
                col.at[other], got2.at[z],
                c_sem.at[0], c_sem.at[1], device_id=device, device_id_type=MESH).start()

        return carry

    lax.fori_loop(1, NZ, send2, 0)
    send_faces(2)

    @pl.when(z < HALF_T)
    def _():
        got2[z] = col[z]
        wait_bytes(got2.at[pl.ds(0, NZ - 1)], c_sem.at[1])
        wait_bytes(got2.at[pl.ds(0, HALF_T - 1)], c_sem.at[0])
        acc = got2[0]
        for k in range(1, NZ):
            acc = acc + got2[k]
        mine[z] = acc

    @pl.when(z >= HALF_T)
    def _():
        wait_bytes(got2.at[pl.ds(0, HALF_T)], c_sem.at[0])

    @pl.when(z < HALF_T)
    def _():
        def send3(k, carry):
            _, device = z_peer(k)
            pltpu.make_async_remote_copy(
                mine.at[z], mine.at[z],
                d_sem.at[0], d_sem.at[1], device_id=device, device_id_type=MESH).start()
            return carry

        lax.fori_loop(1, NZ, send3, 0)

    send_faces(3)

    @pl.when(z < HALF_T)
    def _():
        wait_bytes(mine.at[pl.ds(0, HALF_T - 1)], d_sem.at[1])
        wait_bytes(got2.at[pl.ds(0, NZ - 1)], d_sem.at[0])

    @pl.when(z >= HALF_T)
    def _():
        wait_bytes(mine.at[pl.ds(0, HALF_T)], d_sem.at[1])

    half_bf[...] = mine[...].reshape(HALF_T * 8, CH).astype(BF)

    def send4(k, carry):
        _, device = xy_peer(k)
        pltpu.make_async_remote_copy(
            half_bf, all_bf.at[core, q],
            e_sem.at[0], e_sem.at[1], device_id=device, device_id_type=MESH).start()
        return carry

    lax.fori_loop(1, NXY, send4, 0)
    send_faces(4)
    all_bf[core, q] = half_bf[...]

    for copy in pair:
        copy.wait()
    wait_bytes(recv2.at[peers], r2)
    build_halo(padg, recv2, recv_slot, low2, high2, near_rows, faces)
    back_plane(0)
    back_plane(1)
    back_plane(2)
    back_plane(3)
    span4 = all_bf.at[0, pl.ds(0, NXY - 1)]
    wait_bytes(span4, e_sem.at[1])
    wait_bytes(span4, e_sem.at[0])

    pair1 = pltpu.make_async_remote_copy(
        all_bf.at[core], all_bf.at[core], f_sem.at[0], f_sem.at[1], device_id=partner, device_id_type=MESH)
    pair1.start()
    input_grad[...] = outs[0 : BD * VOX, :].astype(BF)
    wait_bytes(slots2.at[peers], s2)
    pair1.wait()
    for c in range(NCORE):
        for k in range(NXY):
            total[HALF_T * c : HALF_T * (c + 1), 8 * k : 8 * k + 8, :] = (
                all_bf[c, k].astype(F32).reshape(HALF_T, 8, CH))
    total_bf[...] = total[0:TAPS].astype(BF)

def slot_tables(neighbors, me):
    linked = neighbors.T[:4].reshape(4 * BD)
    present = linked >= 0
    owner = jnp.where(present, linked // (BD * SLB), -1)
    position = linked % BD
    key = jnp.arange(4 * BD, dtype=jnp.int32)
    side = key // BD
    wanted = (side + 1 - 2 * (side % 2)) * BD + position
    same = owner[:, None] == owner[None, :]
    send_rank = jnp.sum(same & (key[None, :] < key[:, None]), axis=1, dtype=jnp.int32)
    recv_rank = jnp.sum(same & (wanted[None, :] < wanted[:, None]), axis=1, dtype=jnp.int32)
    send_slot = jnp.where(present, owner * 2 + send_rank, -1)
    recv_slot = jnp.where(present, owner * 2 + recv_rank, 2 * me)
    slot = jnp.arange(SLOTS, dtype=jnp.int32)
    face = side * BP + key - side * BD
    source = jnp.sum(jnp.where(send_slot[None, :] == slot[:, None], face[None, :], 0), axis=1, dtype=jnp.int32)
    return source, recv_slot


def shards(features, weight, cotangent, occupancy, neighbors):
    source, recv_slot = slot_tables(neighbors, lax.axis_index("region"))
    feat = features.reshape(BD * VOX, CH)
    cot = cotangent.reshape(BD * VOX, CH)
    w = weight.reshape(TAPS * CH, CH)

    dma = pltpu.SemaphoreType.DMA
    brick_rows = pltpu.VMEM((BP * VOX, CH), F32)
    pad_shape = pltpu.VMEM((6, 6, 6, BP, CH), BF)
    slot_shape = pltpu.VMEM((SLOTS, 16, CH), BF)
    plane_shape = pltpu.VMEM((4, 4, BP, CH), BF)
    half_shape = pltpu.VMEM((HALF_T, CH, CH), F32)
    tile_shape = pltpu.VMEM((HALF_T, 8, CH), F32)
    output, input_grad, total = pl.pallas_call(
        section_kernel,
        out_shape=(vmem((BD * VOX, CH), BF), vmem((BD * VOX, CH), BF), vmem((TAPS, CH, CH), BF)),
        in_specs=[IN_HBM] * 3 + [IN_VMEM] * 2 + [IN_SMEM] * 2,
        out_specs=(IN_VMEM,) * 3,
        scratch_shapes=[
            pltpu.VMEM((BD * VOX, CH), BF), pltpu.VMEM((BD * VOX, CH), BF), pltpu.VMEM((TAPS * CH, CH), BF),
            pltpu.VMEM((4, BP, 16), F32), pltpu.VMEM((TPAD, CH, CH), F32),
            pltpu.VMEM((8, CH), jnp.int32), dma((3,)),
            pad_shape, pad_shape, pltpu.VMEM((9 * 512, 256), BF), pltpu.VMEM((9 * 512, 256), BF),
            brick_rows, brick_rows, brick_rows,
            pltpu.VMEM((4 * BP, 16, CH), F32),
            slot_shape, slot_shape, slot_shape, slot_shape,
            plane_shape, plane_shape, plane_shape, plane_shape,
            pltpu.VMEM((CH, BP * VOX), BF),
            pltpu.VMEM((TPAD, CH, CH), F32),
            half_shape, tile_shape, tile_shape,
            pltpu.VMEM((HALF_T * 8, CH), BF),
            pltpu.VMEM((NCORE, NXY, HALF_T * 8, CH), BF),
            half_shape,
            pltpu.VMEM((NXY, HALF_T, 8, CH), F32),
            pltpu.VMEM((NZ, 8, CH), F32),
            dma, dma, dma((2,)), dma((2,)), dma, dma, dma((2,)), dma((2,)),
        ] + [dma((2,))] * 6,
        compiler_params=params(collective_id=0, has_side_effects=True),
        name="section",
    )(feat, cot, w, occupancy, neighbors.T, source, recv_slot)

    weight_grad = total.astype(F32) * (BD * REG * SLB * float(VOX)) ** -0.5
    return output.reshape(features.shape), input_grad.reshape(features.shape), weight_grad


def solution(mesh):
    return jax.shard_map(
        shards,
        mesh=mesh,
        in_specs=(
            P(("region", "slab"), None, None, None, None),
            P(),
            P(("region", "slab"), None, None, None, None),
            P(("region", "slab"), None),
            P(("region", "slab"), None),
        ),
        out_specs=(
            P(("region", "slab"), None, None, None, None),
            P(("region", "slab"), None, None, None, None),
            P(),
        ),
        check_vma=False,
    )
```
